256 devices in a mesh: rep: 32 (over z, x_lo, core), shard: 8 (over y, x_hi).
Axes of the slice: x: 4 (x_hi: 2, x_lo: 2; x = x_hi * 2 + x_lo), y: 4, z: 8, core: 2. Of those that a mesh axis runs over, the one named last changes fastest.
Arguments:
- tokens: bfloat16 [32, 2048, 5120], P('rep', 'shard'), may hold values from -6 to 6
- cotangent: bfloat16 [32, 2048, 1024], P('rep', 'shard'), may hold values from -6 to 6
- weight: bfloat16 [5120, 1024], P('shard'), may hold values from -0.078125 to 0.078125
- momentum: float32 [32, 5120, 1024], P('rep', 'shard'), may hold values from -6 to 6
- gain: float32 [1024], replicated, may hold values from 0.1 to 1.9
- band: int32 [640], replicated, may hold values from 0 to 2015, as said below
Outputs:
- input_grad: bfloat16 [32, 2048, 5120], P('rep', 'shard')
- residue: float32 [32, 5120, 1024], P('rep', 'shard')
- update: bfloat16 [5120, 1024], P('shard')
The draws below stay inside these ranges and needn't reach their ends.
Inputs may be any that keep to these rules, and one draw needn't show every extreme that they name: `band`: 640 distinct positions u * 64 + v with u and v both below 32, used for every block.
All inputs are finite; a program needn't handle non-finite values.
Results may differ from the reference program's by a relative error of at most 0.015.
Values may be sent and summed in bfloat16 or wider, within the bound.
No kernel may reach another device: no remote copies, remote signals or barrier semaphores. Data moves between devices by JAX's collectives and lax.ppermute only.
A program may use at most 128 MiB of HBM per device.

```python
import math
import jax
import jax.numpy as jnp
from jax import lax

D = 5120
KV = 1024
TOK_DEV = 256
BAND = 640
REPLICAS = 32
REP_TOK = 2048
N_SHARD = 8


def draw_band(key, part):
    key = jax.random.fold_in(key, 7)
    middle = jax.random.permutation(key, 1022)[:BAND - 2] + 1
    order = jnp.concatenate([jnp.zeros((1,), jnp.int32), middle.astype(jnp.int32), jnp.full((1,), 1023, jnp.int32)])
    return (order // 32 * 64 + order % 32).astype(jnp.int32)


def block_scale(key, extent, split, smallest, high):
    def one(dim, blocks):
        steps = jax.random.uniform(jax.random.fold_in(jax.random.fold_in(key, 6), dim), (blocks,), jnp.float32, smallest / len(split), high / len(split))
        return jnp.repeat(jnp.exp(steps), extent[dim] // blocks).reshape((-1,) + (1,) * (len(extent) - dim - 1))

    level = one(*split[0])
    for cut in split[1:]:
        level = level * one(*cut)
    return level


def normal_values(key, dims, width, bound, split=(), kind=jnp.bfloat16):
    array = width * jax.random.normal(key, dims, jnp.float32)
    if split:
        array = array * block_scale(key, dims, split, -0.22, 0.18)
    return jnp.clip(array, -bound, bound).astype(kind)


def setup_inputs(seed: int = 0) -> dict:
    seeds = jax.random.split(jax.random.key(seed), 7)
    tokens = normal_values(seeds[0], (REPLICAS, REP_TOK, D), 1.0, 6.0, ((0, 32), (1, 8)))
    cotangent = normal_values(seeds[1], (REPLICAS, REP_TOK, KV), 1.0, 6.0, ((0, 32), (1, 8)))
    weight = normal_values(seeds[2], (D, KV), D ** -0.5, 0.078125, ((0, 8),))
    momentum = normal_values(seeds[3], (REPLICAS, D, KV), 1.0, 6.0, ((0, 32), (1, 8)), jnp.float32)
    gain = jnp.clip(1.0 + 0.18 * jax.random.normal(seeds[4], (KV,), jnp.float32), 0.1, 1.9)
    band = draw_band(jax.random.fold_in(seeds[6], 71), 0)
    return dict(tokens=tokens, cotangent=cotangent, weight=weight, momentum=momentum, gain=gain, band=band)


norm_epsilon = 1e-06
block_epsilon = 1e-06
decay_rate = 0.999
step_rate = 0.02

def cosine_table():
    freq = jnp.arange(64, dtype=jnp.float32)
    angle = math.pi * (2.0 * freq[None, :] + 1.0) * freq[:, None] / 128.0
    factor = jnp.where(freq[:, None] == 0.0, math.sqrt(1.0 / 64.0), math.sqrt(2.0 / 64.0))
    return (factor * jnp.cos(angle)).astype(jnp.float32)

def select_table(band):
    return (band[None, :] == jnp.arange(4096, dtype=jnp.int32)[:, None]).astype(jnp.float32)

def forward_coeffs(matrix, table):
    row_count, col_count = matrix.shape
    blocks = matrix.reshape(row_count // 64, 64, col_count // 64, 64)
    coeffs = jnp.einsum('ua,iajb,vb->ijuv', table, blocks, table, precision=lax.Precision.HIGHEST)
    return coeffs.reshape(-1, 4096)

def inverse_coeffs(coeffs, table, row_count, col_count):
    square = coeffs.reshape(row_count // 64, col_count // 64, 64, 64)
    blocks = jnp.einsum('ua,ijuv,vb->iajb', table, square, table, precision=lax.Precision.HIGHEST)
    return blocks.reshape(row_count, col_count)

def band_product(coeffs, select):
    return jnp.dot(coeffs, select, precision=lax.Precision.HIGHEST)

def band_spread(picked, select):
    return lax.dot_general(picked, select, (((1,), (1,)), ((), ())), precision=lax.Precision.HIGHEST)

def block_normalize(matrix):
    row_count, col_count = matrix.shape
    blocks = matrix.reshape(row_count // 64, 64, col_count // 64, 64)
    mean_square = lax.optimization_barrier(jnp.mean(blocks * blocks, axis=(1, 3), keepdims=True))
    return (blocks * lax.rsqrt(mean_square + block_epsilon)).reshape(row_count, col_count)

def key_gradient(projected, upstream, gain):
    mean_square = lax.optimization_barrier(jnp.mean(projected * projected, axis=-1, keepdims=True))
    inverse = lax.rsqrt(mean_square + norm_epsilon)
    scaled = upstream.astype(jnp.float32) * gain.astype(jnp.float32)[None, :]
    projection = lax.optimization_barrier(jnp.mean(scaled * projected, axis=-1, keepdims=True))
    key_grad = inverse * (scaled - projected * inverse * inverse * projection)
    return key_grad.astype(jnp.bfloat16)

def reference(tokens, cotangent, weight, momentum, gain, band):
    table = cosine_table()
    select = select_table(band)

    def per_replica(inputs):
        activations, upstream, previous = inputs
        projected = jnp.dot(activations, weight, preferred_element_type=jnp.float32)
        key_grad = key_gradient(projected, upstream, gain)
        input_grad = lax.dot_general(key_grad, weight, (((1,), (1,)), ((), ())), preferred_element_type=jnp.float32).astype(jnp.bfloat16)
        token_blocks = activations.reshape(N_SHARD, TOK_DEV, D).astype(jnp.float32)
        grad_blocks = key_grad.reshape(N_SHARD, TOK_DEV, KV).astype(jnp.float32)
        partials = jnp.einsum('sta,stb->sab', token_blocks, grad_blocks, precision=lax.Precision.HIGHEST)
        partials = lax.optimization_barrier(partials.astype(jnp.bfloat16)).astype(jnp.float32)
        gradient = lax.optimization_barrier(jnp.sum(partials, axis=0))
        blended = decay_rate * previous + step_rate * gradient
        coeffs = forward_coeffs(blended, table)
        picked = band_product(coeffs, select)
        residue = blended - inverse_coeffs(band_spread(picked, select), table, D, KV)
        return (input_grad, residue, picked)
    input_grad, residue, picked = lax.map(per_replica, (tokens, cotangent, momentum))
    summed = lax.optimization_barrier(jnp.sum(picked, axis=0))
    combined = inverse_coeffs(band_spread(summed, select), table, D, KV)
    update = block_normalize(combined).astype(jnp.bfloat16)
    return (input_grad, residue, update)
```

```python
import math

import jax
import jax.numpy as jnp
import numpy as np
from jax import lax
from jax.experimental import pallas as pl
from jax.experimental.pallas import tpu as pltpu
from jax.sharding import PartitionSpec as P

norm_epsilon = 1e-06
block_epsilon = 1e-06
decay_rate = 0.999
step_rate = 0.02

Z, XL, CORE, Y, XH = 8, 2, 2, 4, 2
X = XL * XH
TOK, D, KV, ROWS = 256, 5120, 1024, 640
HALF = KV // 2
bf16, f32 = jnp.bfloat16, jnp.float32
ANY = pl.BlockSpec(memory_space=pl.ANY)
VMEM = pl.BlockSpec(memory_space=pltpu.VMEM)
SMEM = pl.BlockSpec(memory_space=pltpu.SMEM)


def device_index(z, x, c, y):
    z, x, y = z % Z, x % X, y % Y
    return (((z * XL + x % XL) * CORE + c) * Y + y) * XH + x // XL


def pull(value, source):
    pairs = []
    for z in range(Z):
        for x in range(X):
            for c in range(CORE):
                for y in range(Y):
                    found = source(z, x, c, y)
                    if found is not None:
                        pairs.append((device_index(*found), device_index(z, x, c, y)))
    return lax.ppermute(value, ("rep", "shard"), pairs)


def from_shard(dy, dx):
    return lambda z, x, c, y: (z, x + 2 * dx, c, y + dy)


def split_bf16(table):
    high = table.astype(bf16)
    low = (table - high.astype(np.float32)).astype(bf16)
    return np.stack([high, low])


def dct_tables():
    freq = np.arange(64, dtype=np.float64)
    angle = math.pi * (2.0 * freq[None, :] + 1.0) * freq[:, None] / 128.0
    factor = np.where(freq[:, None] == 0.0, math.sqrt(1.0 / 64.0), math.sqrt(2.0 / 64.0))
    table = (factor * np.cos(angle))[:32].astype(np.float32)
    left = np.kron(np.eye(2, dtype=np.float32), table)
    right = np.kron(np.eye(4, dtype=np.float32), table.T)
    return split_bf16(left), split_bf16(right)


def split(value):
    high = value.astype(bf16)
    return high, (value - high.astype(f32)).astype(bf16)


def mm(a, b):
    return jnp.dot(a, b, preferred_element_type=f32)


def mm_left(table, value):
    high, low = split(value)
    return mm(table[0], high) + mm(table[0], low) + mm(table[1], high)


def mm_right(value, table):
    high, low = split(value)
    return mm(high, table[0]) + mm(low, table[0]) + mm(high, table[1])


def params(limit=48):
    return pltpu.CompilerParams(vmem_limit_bytes=limit * 1024 * 1024)


def cut_columns(value, indices, width, count, transposed=False):
    rows = value.shape[0]

    def kernel(index_ref, *refs):
        for k in range(count):
            block = refs[k][...]
            refs[count + k][...] = block.T if transposed else block

    shape = (width, rows) if transposed else (rows, width)
    return pl.pallas_call(
        kernel,
        grid_spec=pltpu.PrefetchScalarGridSpec(
            num_scalar_prefetch=1,
            grid=(1,),
            in_specs=[pl.BlockSpec((rows, width), lambda i, s, k=k: (0, s[k])) for k in range(count)],
            out_specs=[pl.BlockSpec(shape, lambda i, s: (0, 0))] * count,
        ),
        out_shape=[jax.ShapeDtypeStruct(shape, value.dtype)] * count,
        compiler_params=params(),
        cost_estimate=pl.CostEstimate(flops=0, bytes_accessed=4 * rows * width * count, transcendentals=0),
    )(indices, *([value] * count))


def project(tokens, shards, pieces, total=None):
    count = len(pieces)

    def kernel(shard_ref, *refs):
        toks, ws = refs[:count], refs[count : 2 * count]
        acc = mm(toks[0][...], ws[0][...])
        for k in range(1, count):
            acc += mm(toks[k][...], ws[k][...])
        if total is not None:
            acc += refs[2 * count][...]
        refs[-1][...] = acc

    token_specs = [pl.BlockSpec((TOK, ROWS), lambda i, s, k=k: (0, s[k])) for k in range(count)]
    piece_specs = [pl.BlockSpec(p.shape, lambda i, s: (0, 0)) for p in pieces]
    full = pl.BlockSpec((TOK, HALF), lambda i, s: (0, 0))
    extra = [] if total is None else [total]
    return pl.pallas_call(
        kernel,
        grid_spec=pltpu.PrefetchScalarGridSpec(
            num_scalar_prefetch=1,
            grid=(1,),
            in_specs=token_specs + piece_specs + [full] * len(extra),
            out_specs=full,
        ),
        out_shape=jax.ShapeDtypeStruct((TOK, HALF), f32),
        compiler_params=params(),
        cost_estimate=pl.CostEstimate(
            flops=2 * TOK * ROWS * HALF * count,
            bytes_accessed=count * (TOK * ROWS + ROWS * HALF) * 2,
            transcendentals=0,
        ),
    )(shards, *([tokens] * count), *pieces, *extra)


def key_gradient(parity, first, second, cotangent, gain):
    def kernel(parity_ref, a_ref, b_ref, ca_ref, cb_ref, ga_ref, gb_ref, out_ref):
        p = parity_ref[0]
        a, b = a_ref[...], b_ref[...]
        sa = ca_ref[...].astype(f32) * ga_ref[...]
        sb = cb_ref[...].astype(f32) * gb_ref[...]
        square = jnp.sum(a * a, axis=-1, keepdims=True) + jnp.sum(b * b, axis=-1, keepdims=True)
        cross = jnp.sum(sa * a, axis=-1, keepdims=True) + jnp.sum(sb * b, axis=-1, keepdims=True)
        inverse = lax.rsqrt(square * (1.0 / KV) + norm_epsilon)
        factor = inverse * inverse * (cross * (1.0 / KV))
        out_ref[:, pl.ds(pl.multiple_of(p * HALF, HALF), HALF)] = (inverse * (sa - a * factor)).astype(bf16)
        out_ref[:, pl.ds(pl.multiple_of((1 - p) * HALF, HALF), HALF)] = (inverse * (sb - b * factor)).astype(bf16)

    full = pl.BlockSpec((TOK, HALF), lambda i, s: (0, 0))
    return pl.pallas_call(
        kernel,
        grid_spec=pltpu.PrefetchScalarGridSpec(
            num_scalar_prefetch=1,
            grid=(1,),
            in_specs=[
                full,
                full,
                pl.BlockSpec((TOK, HALF), lambda i, s: (0, s[0])),
                pl.BlockSpec((TOK, HALF), lambda i, s: (0, 1 - s[0])),
                pl.BlockSpec((1, HALF), lambda i, s: (0, s[0])),
                pl.BlockSpec((1, HALF), lambda i, s: (0, 1 - s[0])),
            ],
            out_specs=pl.BlockSpec((TOK, KV), lambda i, s: (0, 0)),
        ),
        out_shape=jax.ShapeDtypeStruct((TOK, KV), bf16),
        compiler_params=params(),
        cost_estimate=pl.CostEstimate(flops=10 * TOK * KV, bytes_accessed=TOK * KV * 8, transcendentals=TOK),
    )(parity, first, second, cotangent, cotangent, gain, gain)


def token_gradient(scalars, key_grad, own, near, far):
    pieces = [w for pair in near + far for w in pair]
    count = len(pieces)

    def kernel(s_ref, key_ref, own_ref, *refs):
        out_ref = refs[-1]
        p = s_ref[0]
        ka = key_ref[:, pl.ds(pl.multiple_of(p * HALF, HALF), HALF)]
        kb = key_ref[:, pl.ds(pl.multiple_of((1 - p) * HALF, HALF), HALF)]

        def against(k, w):
            return lax.dot_general(k, w, (((1,), (1,)), ((), ())), preferred_element_type=f32)

        def store(slot, value):
            at = pl.multiple_of(s_ref[slot] * ROWS, 128)
            out_ref[:, pl.ds(at, ROWS)] = value.astype(bf16)

        for k in range(3):
            store(1 + k, against(ka, refs[2 + 2 * k][...]) + against(kb, refs[3 + 2 * k][...]))
            store(4 + k, against(ka, refs[10 + 2 * k][...]) + against(kb, refs[11 + 2 * k][...]))
        store(7, against(key_ref[...], own_ref[...]))
        store(
            8,
            against(ka, refs[0][...]) + against(kb, refs[1][...])
            + against(ka, refs[8][...]) + against(kb, refs[9][...]),
        )

    return pl.pallas_call(
        kernel,
        in_specs=[SMEM] + [VMEM] * (2 + count),
        out_specs=VMEM,
        out_shape=jax.ShapeDtypeStruct((TOK, D), bf16),
        compiler_params=params(),
        cost_estimate=pl.CostEstimate(flops=2 * TOK * KV * D, bytes_accessed=(KV * D + TOK * D) * 2, transcendentals=0),
    )(scalars, key_grad, own, *pieces)


def against(a, b):
    return lax.dot_general(a, b, (((1,), (1,)), ((), ())), preferred_element_type=f32)


def across(a, b):
    return lax.dot_general(a, b, (((0,), (0,)), ((), ())), preferred_element_type=f32)


def to_corner(value, left, right):
    narrow = mm_right(value, right)
    return jnp.concatenate([mm_left(left, narrow[128 * i : 128 * i + 128]) for i in range(5)], axis=0)


def from_corner(corner, left, right):
    high, low = split(corner)
    blocks = []
    for i in range(5):
        h, l = high[64 * i : 64 * i + 64], low[64 * i : 64 * i + 64]
        blocks.append(across(left[0], h) + across(left[0], l) + across(left[1], h))
    high, low = split(jnp.concatenate(blocks, axis=0))
    return against(high, right[0]) + against(low, right[0]) + against(high, right[1])


def blend(tokens, keys, momentum, mask, left, right, after):
    count = len(keys)
    width = 256

    def kernel(*refs):
        toks, ks = refs[:count], refs[count : 2 * count]
        momentum_ref, mask_ref, left_ref, right_ref, _, blended_ref, corner_ref = refs[2 * count :]
        t = jnp.concatenate([ref[...] for ref in toks], axis=1)
        k = jnp.concatenate([ref[...] for ref in ks], axis=0)
        blended = decay_rate * momentum_ref[...] + step_rate * mm(t, k)
        blended_ref[...] = blended
        corner_ref[0] = to_corner(blended, left_ref[...], right_ref[...]) * mask_ref[...]

    specs = [pl.BlockSpec((ROWS, TOK), lambda i: (0, 0))] * count
    specs += [pl.BlockSpec((TOK, width), lambda i: (0, i))] * count
    specs += [
        pl.BlockSpec((ROWS, width), lambda i: (0, i)),
        pl.BlockSpec(mask.shape, lambda i: (0, 0)),
        pl.BlockSpec(left.shape, lambda i: (0, 0, 0)),
        pl.BlockSpec(right.shape, lambda i: (0, 0, 0)),
        ANY,
    ]
    return pl.pallas_call(
        kernel,
        grid=(KV // width,),
        in_specs=specs,
        out_specs=[
            pl.BlockSpec((ROWS, width), lambda i: (0, i)),
            pl.BlockSpec((1, 320, 128), lambda i: (i, 0, 0)),
        ],
        out_shape=[jax.ShapeDtypeStruct((ROWS, KV), f32), jax.ShapeDtypeStruct((4, 320, 128), f32)],
        compiler_params=params(),
        cost_estimate=pl.CostEstimate(
            flops=2 * TOK * count * KV * ROWS, bytes_accessed=ROWS * KV * 8 + count * TOK * (ROWS + KV) * 2, transcendentals=0
        ),
    )(*tokens, *keys, momentum, mask, left, right, after)


def remove_corner(blended, corner, left, right):
    def kernel(blended_ref, corner_ref, left_ref, right_ref, out_ref):
        out_ref[...] = blended_ref[...] - from_corner(corner_ref[0], left_ref[...], right_ref[...])

    return pl.pallas_call(
        kernel,
        grid=(4,),
        in_specs=[
            pl.BlockSpec((ROWS, 256), lambda i: (0, i)),
            pl.BlockSpec((1, 320, 128), lambda i: (i, 0, 0)),
            pl.BlockSpec(left.shape, lambda i: (0, 0, 0)),
            pl.BlockSpec(right.shape, lambda i: (0, 0, 0)),
        ],
        out_specs=pl.BlockSpec((ROWS, 256), lambda i: (0, i)),
        out_shape=jax.ShapeDtypeStruct((ROWS, KV), f32),
        compiler_params=params(),
        cost_estimate=pl.CostEstimate(flops=2 * ROWS * KV * 256, bytes_accessed=ROWS * KV * 8, transcendentals=0),
    )(blended, corner, left, right)


def normalized_update(me, quarters, left, right, ones):
    def kernel(me_ref, a, b, c, d, left_ref, right_ref, ones_ref, out_ref):
        left, right, ones = left_ref[...], right_ref[...], ones_ref[...]
        for k, ref in enumerate((a, b, c, d)):
            corner = ref[...].astype(f32)
            energy = jnp.sum((corner * corner).reshape(10, 32, 128), axis=1)
            high, low = split(energy)
            energy = mm(high, ones) + mm(low, ones)
            scale = lax.rsqrt(energy * (1.0 / 4096.0) + block_epsilon)
            corner = (corner.reshape(10, 32, 128) * scale[:, None, :]).reshape(320, 128)
            columns = pl.ds(pl.multiple_of((me_ref[0] ^ k) * 256, 256), 256)
            out_ref[:, columns] = from_corner(corner, left, right).astype(bf16)

    return pl.pallas_call(
        kernel,
        in_specs=[SMEM] + [VMEM] * 7,
        out_specs=VMEM,
        out_shape=jax.ShapeDtypeStruct((ROWS, KV), bf16),
        compiler_params=params(),
    )(me, *quarters, left, right, ones)


def per_device(tokens, cotangent, weight, momentum, gain, band):
    tokens, cotangent, momentum = tokens[0], cotangent[0], momentum[0]
    rep, shard = lax.axis_index("rep"), lax.axis_index("shard")
    z, core = rep // 4, rep % 2
    y, xh = shard // 2, shard % 2
    parity = (z % 2).astype(jnp.int32)

    def shard_at(dy, dx):
        return (((y + dy) % 4) * 2 + (xh ^ dx)).astype(jnp.int32)

    left, right = (jnp.asarray(t) for t in dct_tables())
    ones = jnp.asarray(np.kron(np.eye(4), np.ones((32, 32))).astype(np.float32), bf16)
    corner_positions = (jnp.arange(32)[:, None] * 64 + jnp.arange(32)[None, :]).reshape(1024, 1)
    mask = jnp.any(corner_positions == band[None, :], axis=1).astype(f32).reshape(32, 32)
    mask = jnp.tile(mask, (10, 4))

    own_halves = cut_columns(weight, jnp.stack([parity, 1 - parity]), HALF, 2)

    def near_source(dy):
        def source(z, x, c, y):
            if c == 0:
                return None if dy == 0 else (z, x, c, y + dy)
            return (z, 3 - x, c, y + dy)

        return source

    def z_source(dy):
        def source(z, x, c, y):
            if c == 0:
                return None if dy == 0 else (z + 1, x, c, y)
            return (z - 1, x, c, y)

        return source

    def core_source(dy):
        return lambda z, x, c, y: None if dy == 0 and c == 1 else (z, x, 1 - c, y)

    first = [pull(own_halves[0], near_source(dy)) for dy in range(4)]
    second = [pull(first[dy], z_source(dy)) for dy in range(4)]
    far_first = [pull(first[dy], core_source(dy)) for dy in range(4)]
    far_second = [pull(second[dy], core_source(dy)) for dy in range(4)]

    away = [(dy, dx) for dy in range(4) for dx in range(2)][1:]
    mine, *sent = cut_columns(tokens, jnp.stack([shard_at(*a) for a in [(0, 0)] + away]), ROWS, 8, transposed=True)
    arrived = {((-dy) % 4, dx): pull(sent[k], from_shard(-dy, dx)) for k, (dy, dx) in enumerate(away)}

    near_shards = jnp.stack([shard_at(0, 1), *[shard_at(dy, core) for dy in range(1, 4)], shard_at(0, 0)])
    far_shards = jnp.stack([shard_at(0, 1), *[shard_at(dy, 1 - core) for dy in range(1, 4)]])
    half_a = project(tokens, near_shards, first + [own_halves[0]])
    half_b = project(tokens, near_shards, second + [own_halves[1]])
    half_a = project(tokens, far_shards, far_first, half_a)
    half_b = project(tokens, far_shards, far_second, half_b)
    key_grad = key_gradient(parity[None], half_a, half_b, cotangent, gain[None])

    keys = {(0, 0): key_grad}
    keys[0, 1] = pull(key_grad, from_shard(0, 1))
    for dy in (1, 3, 2):
        keys[dy, 0] = pull(key_grad, from_shard(dy, 0))
    keys[1, 1] = pull(keys[0, 1], from_shard(1, 0))
    keys[3, 1] = pull(keys[0, 1], from_shard(3, 0))
    keys[2, 1] = pull(keys[2, 0], from_shard(0, 1))

    scalars = jnp.stack(
        [parity, *[shard_at(dy, core) for dy in range(1, 4)], *[shard_at(dy, 1 - core) for dy in range(1, 4)],
         shard_at(0, 0), shard_at(0, 1)]
    )
    input_grad = token_gradient(
        scalars, key_grad, weight, list(zip(first, second)), list(zip(far_first, far_second))
    )

    blended, corner = blend(
        [mine] + [arrived[a] for a in away],
        [key_grad] + [keys[a] for a in away],
        momentum, mask, left, right, input_grad,
    )
    residue = remove_corner(blended, corner, left, right)

    me = (rep % 4).astype(jnp.int32)

    def group_source(k):
        return lambda z, x, c, y: (z, x ^ (k // 2), c ^ (k % 2), y)

    def quarter(k):
        return lax.dynamic_index_in_dim(corner, me ^ k, 0, keepdims=False)

    total = quarter(0)
    for part in [pull(quarter(k).astype(bf16), group_source(k)) for k in (2, 3, 1)]:
        total = total + part.astype(f32)
    summed = total.astype(bf16)
    for bit in (1, 2, 4):
        other = pull(summed, lambda z, x, c, y: (z ^ bit, x, c, y))
        summed = (summed.astype(f32) + other.astype(f32)).astype(bf16)
    quarters = [summed] + [pull(summed, group_source(k)) for k in (1, 2, 3)]
    update = normalized_update(me[None], quarters, left, right, ones)
    return (input_grad[None], residue[None], update)


def solution(mesh):
    return jax.shard_map(
        per_device,
        mesh=mesh,
        in_specs=(
            P("rep", "shard", None),
            P("rep", "shard", None),
            P("shard", None),
            P("rep", "shard", None),
            P(),
            P(),
        ),
        out_specs=(P("rep", "shard", None), P("rep", "shard", None), P("shard", None)),
        check_vma=False,
    )
```

```python
import math

import jax
import jax.numpy as jnp
import numpy as np
from jax import lax
from jax.experimental import pallas as pl
from jax.experimental.pallas import tpu as pltpu
from jax.sharding import PartitionSpec as P

norm_epsilon = 1e-06
block_epsilon = 1e-06
decay_rate = 0.999
step_rate = 0.02

Z, XL, CORE, Y, XH = 8, 2, 2, 4, 2
X = XL * XH
TOK, D, KV, ROWS = 256, 5120, 1024, 640
HALF = KV // 2
bf16, f32 = jnp.bfloat16, jnp.float32
PARITY, IS_CORE1, ME, NEAR, FAR, AWAY_AT, OTHER_HALF = 0, 1, 2, 3, 7, 11, 19
AWAY = [(0, 0), (1, 0), (3, 0), (0, 1), (2, 0), (1, 1), (3, 1), (2, 1)]
STEPS = ((1, 0), (3, 1), (2, 3), (0, 2))
ANY = pl.BlockSpec(memory_space=pl.ANY)
VMEM = pl.BlockSpec(memory_space=pltpu.VMEM)
SMEM = pl.BlockSpec(memory_space=pltpu.SMEM)


def device_index(z, x, c, y):
    z, x, y = z % Z, x % X, y % Y
    return (((z * XL + x % XL) * CORE + c) * Y + y) * XH + x // XL


def pull(value, source):
    pairs = []
    for z in range(Z):
        for x in range(X):
            for c in range(CORE):
                for y in range(Y):
                    found = source(z, x, c, y)
                    if found is not None:
                        pairs.append((device_index(*found), device_index(z, x, c, y)))
    return lax.ppermute(value, ("rep", "shard"), pairs)


def from_shard(dy, dx):
    return lambda z, x, c, y: (z, x + 2 * dx, c, y + dy)


def split_bf16(table):
    high = table.astype(bf16)
    low = (table - high.astype(np.float32)).astype(bf16)
    return np.stack([high, low])


def dct_tables():
    freq = np.arange(64, dtype=np.float64)
    angle = math.pi * (2.0 * freq[None, :] + 1.0) * freq[:, None] / 128.0
    factor = np.where(freq[:, None] == 0.0, math.sqrt(1.0 / 64.0), math.sqrt(2.0 / 64.0))
    table = (factor * np.cos(angle))[:32].astype(np.float32)
    left = np.kron(np.eye(2, dtype=np.float32), table)
    right = np.kron(np.eye(4, dtype=np.float32), table.T)
    return split_bf16(left), split_bf16(right)


def split(value):
    high = value.astype(bf16)
    return high, (value - high.astype(f32)).astype(bf16)


def mm(a, b):
    return jnp.dot(a, b, preferred_element_type=f32)


def mm_left(table, value):
    high, low = split(value)
    return mm(table[0], high) + mm(table[0], low) + mm(table[1], high)


def mm_right(value, table):
    high, low = split(value)
    return mm(high, table[0]) + mm(low, table[0]) + mm(high, table[1])


def params(limit=56):
    return pltpu.CompilerParams(vmem_limit_bytes=limit * 1024 * 1024)


def cut_columns(info, value, slots, width, transposed=False, joined=False, after=()):
    rows, count = value.shape[0], len(slots)

    def kernel(info_ref, *refs):
        for k in range(count):
            block = refs[k][...]
            block = block.T if transposed else block
            if joined:
                refs[-1][:, width * k : width * k + width] = block
            else:
                refs[count + len(after) + k][...] = block

    shape = (rows, width * count) if joined else (width, rows) if transposed else (rows, width)
    outs = 1 if joined else count
    return pl.pallas_call(
        kernel,
        grid_spec=pltpu.PrefetchScalarGridSpec(
            num_scalar_prefetch=1,
            grid=(1,),
            in_specs=[pl.BlockSpec((rows, width), lambda i, s, k=k: (0, s[k])) for k in slots] + [ANY] * len(after),
            out_specs=[pl.BlockSpec(shape, lambda i, s: (0, 0))] * outs,
        ),
        out_shape=[jax.ShapeDtypeStruct(shape, value.dtype)] * outs,
        compiler_params=params(),
        cost_estimate=pl.CostEstimate(flops=0, bytes_accessed=4 * rows * width * count, transcendentals=0),
    )(info, *([value] * count), *after)


def column_half(ref, p):
    return ref[:, pl.ds(pl.multiple_of(p * HALF, HALF), HALF)]


def project(info, tokens, others, own, first, second, after):
    def kernel(info_ref, t_ref, o_ref, own_ref, *refs):
        ws, outs = refs[:8], refs[8 + len(after) : 10 + len(after)]
        toks, other, weights, sems = refs[10 + len(after) :]
        p, core = info_ref[PARITY], info_ref[IS_CORE1]
        copies = []

        def start(source, target):
            copies.append(pltpu.make_async_copy(source, target, sems.at[len(copies)]))
            copies[-1].start()

        start(o_ref, other)
        for k in range(4):
            at = pl.ds(pl.multiple_of(info_ref[NEAR + k] * ROWS, 128), ROWS)
            start(t_ref.at[:, at], toks.at[k])
        for k in range(4):
            for h in range(2):
                start(ws[4 * h + k], weights.at[2 * k + h])
        for copy in copies[:5]:
            copy.wait()
        sums = [[None, None], [None, None]]
        for k in range(4):
            for h in range(2):
                copies[5 + 2 * k + h].wait()
                w = weights[2 * k + h]
                if k == 3:
                    w = jnp.where(core == 0, column_half(own_ref, p if h == 0 else 1 - p), w)
                for n, t in enumerate((toks[k], other[:, ROWS * k : ROWS * k + ROWS])):
                    term = mm(t, w)
                    sums[n][h] = term if k == 0 else sums[n][h] + term
        for n in range(2):
            for h in range(2):
                outs[n][:, HALF * h : HALF * h + HALF] = sums[n][h]

    return pl.pallas_call(
        kernel,
        in_specs=[SMEM, ANY, ANY, VMEM] + [ANY] * (8 + len(after)),
        out_specs=[VMEM] * 2,
        out_shape=[jax.ShapeDtypeStruct((TOK, KV), f32)] * 2,
        scratch_shapes=[
            pltpu.VMEM((4, TOK, ROWS), bf16),
            pltpu.VMEM((TOK, 4 * ROWS), bf16),
            pltpu.VMEM((8, ROWS, HALF), bf16),
            pltpu.SemaphoreType.DMA((13,)),
        ],
        compiler_params=params(),
        cost_estimate=pl.CostEstimate(flops=2 * TOK * D * KV, bytes_accessed=(KV * D + TOK * D) * 2, transcendentals=0),
    )(info, tokens, others, own, *first, *second, *after)


def key_gradient(info, mine, arrived, cotangent, gain, after):
    def kernel(s_ref, m_ref, r_ref, ca_ref, cb_ref, ga_ref, gb_ref, *refs):
        out_ref = refs[-1]
        p = s_ref[PARITY]
        both = m_ref[...] + r_ref[...]
        a, b = both[:, :HALF], both[:, HALF:]
        sa = ca_ref[...].astype(f32) * ga_ref[...]
        sb = cb_ref[...].astype(f32) * gb_ref[...]
        square = jnp.sum(a * a, axis=-1, keepdims=True) + jnp.sum(b * b, axis=-1, keepdims=True)
        cross = jnp.sum(sa * a, axis=-1, keepdims=True) + jnp.sum(sb * b, axis=-1, keepdims=True)
        inverse = lax.rsqrt(square * (1.0 / KV) + norm_epsilon)
        factor = inverse * inverse * (cross * (1.0 / KV))
        out_ref[:, pl.ds(pl.multiple_of(p * HALF, HALF), HALF)] = (inverse * (sa - a * factor)).astype(bf16)
        out_ref[:, pl.ds(pl.multiple_of((1 - p) * HALF, HALF), HALF)] = (inverse * (sb - b * factor)).astype(bf16)

    full = pl.BlockSpec((TOK, KV), lambda i, s: (0, 0))
    return pl.pallas_call(
        kernel,
        grid_spec=pltpu.PrefetchScalarGridSpec(
            num_scalar_prefetch=1,
            grid=(1,),
            in_specs=[
                full,
                full,
                pl.BlockSpec((TOK, HALF), lambda i, s: (0, s[PARITY])),
                pl.BlockSpec((TOK, HALF), lambda i, s: (0, 1 - s[PARITY])),
                pl.BlockSpec((1, HALF), lambda i, s: (0, s[PARITY])),
                pl.BlockSpec((1, HALF), lambda i, s: (0, 1 - s[PARITY])),
            ]
            + [ANY] * len(after),
            out_specs=full,
        ),
        out_shape=jax.ShapeDtypeStruct((TOK, KV), bf16),
        compiler_params=params(),
        cost_estimate=pl.CostEstimate(flops=10 * TOK * KV, bytes_accessed=TOK * KV * 12, transcendentals=TOK),
    )(info, mine, arrived, cotangent, cotangent, gain, gain, *after)


def token_gradient(info, key_grad, other_keys, own, first, second, after):
    def kernel(info_ref, k_ref, o_ref, own_ref, *refs):
        ws, outs = refs[:8], refs[8 + len(after) :]
        p, core = info_ref[PARITY], info_ref[IS_CORE1]
        for k in range(4):
            wa, wb = ws[k][...], ws[4 + k][...]
            if k == 3:
                wa = jnp.where(core == 0, column_half(own_ref, p), wa)
                wb = jnp.where(core == 0, column_half(own_ref, 1 - p), wb)
            for keys, out in zip((k_ref, o_ref), outs):
                value = against(column_half(keys, p), wa) + against(column_half(keys, 1 - p), wb)
                out[:, ROWS * k : ROWS * k + ROWS] = value.astype(bf16)

    return pl.pallas_call(
        kernel,
        in_specs=[SMEM] + [VMEM] * 11 + [ANY] * len(after),
        out_specs=[VMEM] * 2,
        out_shape=[jax.ShapeDtypeStruct((TOK, 4 * ROWS), bf16)] * 2,
        compiler_params=params(),
        cost_estimate=pl.CostEstimate(flops=2 * TOK * KV * D, bytes_accessed=(KV * D + TOK * D) * 2, transcendentals=0),
    )(info, key_grad, other_keys, own, *first, *second, *after)


def place_columns(info, mine, arrived):
    def kernel(info_ref, m_ref, r_ref, out_ref):
        for slot, ref in ((NEAR, m_ref), (FAR, r_ref)):
            for k in range(4):
                at = pl.ds(pl.multiple_of(info_ref[slot + k] * ROWS, 128), ROWS)
                out_ref[:, at] = ref[:, ROWS * k : ROWS * k + ROWS]

    return pl.pallas_call(
        kernel,
        in_specs=[SMEM] + [VMEM] * 2,
        out_specs=VMEM,
        out_shape=jax.ShapeDtypeStruct((TOK, D), bf16),
        compiler_params=params(),
        cost_estimate=pl.CostEstimate(flops=0, bytes_accessed=4 * TOK * D, transcendentals=0),
    )(info, mine, arrived)


def against(a, b):
    return lax.dot_general(a, b, (((1,), (1,)), ((), ())), preferred_element_type=f32)


def across(a, b):
    return lax.dot_general(a, b, (((0,), (0,)), ((), ())), preferred_element_type=f32)


def to_corner(value, left, right):
    narrow = mm_right(value, right)
    return jnp.concatenate([mm_left(left, narrow[128 * i : 128 * i + 128]) for i in range(5)], axis=0)


def from_corner(corner, left, right):
    high, low = split(corner)
    blocks = []
    for i in range(5):
        h, l = high[64 * i : 64 * i + 64], low[64 * i : 64 * i + 64]
        blocks.append(across(left[0], h) + across(left[0], l) + across(left[1], h))
    high, low = split(jnp.concatenate(blocks, axis=0))
    return against(high, right[0]) + against(low, right[0]) + against(high, right[1])


def blend(info, tokens, keys, momentum, mask, tables, after):
    count = len(keys)
    width = 256

    def kernel(info_ref, *refs):
        toks, ks = refs[:count], refs[count : 2 * count]
        momentum_ref, mask_ref, left_ref, right_ref, _, blended_ref, corner_ref, *parts = refs[2 * count :]
        t = jnp.concatenate([ref[...] for ref in toks], axis=1)
        k = jnp.concatenate([ref[...] for ref in ks], axis=0)
        blended = decay_rate * momentum_ref[...] + step_rate * mm(t, k)
        blended_ref[...] = blended
        corner = to_corner(blended, left_ref[...], right_ref[...]) * mask_ref[...]
        corner_ref[0] = corner
        for i in range(4):

            @pl.when(pl.program_id(0) == i)
            def _():
                parts[i][...] = corner.astype(parts[i].dtype)

    def whole(a):
        return pl.BlockSpec(a.shape, lambda i, s: (0,) * a.ndim)

    columns = pl.BlockSpec((ROWS, width), lambda i, s: (0, s[ME] ^ i))
    specs = [pl.BlockSpec((ROWS, TOK), lambda i, s: (0, 0))] * count
    specs += [pl.BlockSpec((TOK, width), lambda i, s: (0, s[ME] ^ i))] * count
    specs += [columns, whole(mask), whole(tables[0]), whole(tables[1]), ANY]
    part = pl.BlockSpec((320, 128), lambda i, s: (0, 0))
    return pl.pallas_call(
        kernel,
        grid_spec=pltpu.PrefetchScalarGridSpec(
            num_scalar_prefetch=1,
            grid=(KV // width,),
            in_specs=specs,
            out_specs=[columns, pl.BlockSpec((1, 320, 128), lambda i, s: (s[ME] ^ i, 0, 0))] + [part] * 4,
        ),
        out_shape=[jax.ShapeDtypeStruct((ROWS, KV), f32), jax.ShapeDtypeStruct((4, 320, 128), f32)]
        + [jax.ShapeDtypeStruct((320, 128), t) for t in (f32, bf16, bf16, bf16)],
        compiler_params=params(),
        cost_estimate=pl.CostEstimate(
            flops=2 * TOK * count * KV * ROWS, bytes_accessed=ROWS * KV * 8 + count * TOK * (ROWS + KV) * 2, transcendentals=0
        ),
    )(info, *tokens, *keys, momentum, mask, *tables, after)


def remove_corner(blended, corner, tables):
    def kernel(blended_ref, corner_ref, left_ref, right_ref, out_ref):
        out_ref[...] = blended_ref[...] - from_corner(corner_ref[0], left_ref[...], right_ref[...])

    return pl.pallas_call(
        kernel,
        grid=(4,),
        in_specs=[
            pl.BlockSpec((ROWS, 256), lambda i: (0, i)),
            pl.BlockSpec((1, 320, 128), lambda i: (i, 0, 0)),
            pl.BlockSpec(tables[0].shape, lambda i: (0, 0, 0)),
            pl.BlockSpec(tables[1].shape, lambda i: (0, 0, 0)),
        ],
        out_specs=pl.BlockSpec((ROWS, 256), lambda i: (0, i)),
        out_shape=jax.ShapeDtypeStruct((ROWS, KV), f32),
        compiler_params=params(),
        cost_estimate=pl.CostEstimate(flops=2 * ROWS * KV * 256, bytes_accessed=ROWS * KV * 8, transcendentals=0),
    )(blended, corner, *tables)


def add_parts(own, parts, after):
    def kernel(a, b, c, d, _, out_ref):
        out_ref[...] = (a[...] + b[...].astype(f32) + (c[...].astype(f32) + d[...].astype(f32))).astype(bf16)

    return pl.pallas_call(
        kernel,
        in_specs=[VMEM] * 4 + [ANY],
        out_specs=VMEM,
        out_shape=jax.ShapeDtypeStruct(own.shape, bf16),
        compiler_params=params(),
    )(own, *parts, after)


def normalized_update(info, quarters, tables, ones):
    def kernel(info_ref, a, b, c, d, left_ref, right_ref, ones_ref, out_ref):
        for k, ref in enumerate((a, b, c, d)):
            corner = ref[...].astype(f32)
            energy = jnp.sum((corner * corner).reshape(10, 32, 128), axis=1)
            high, low = split(energy)
            energy = mm(high, ones_ref[...]) + mm(low, ones_ref[...])
            scale = lax.rsqrt(energy * (1.0 / 4096.0) + block_epsilon)
            corner = (corner.reshape(10, 32, 128) * scale[:, None, :]).reshape(320, 128)
            columns = pl.ds(pl.multiple_of((info_ref[ME] ^ k) * 256, 256), 256)
            out_ref[:, columns] = from_corner(corner, left_ref[...], right_ref[...]).astype(bf16)

    return pl.pallas_call(
        kernel,
        in_specs=[SMEM] + [VMEM] * 7,
        out_specs=VMEM,
        out_shape=jax.ShapeDtypeStruct((ROWS, KV), bf16),
        compiler_params=params(),
    )(info, *quarters, *tables, ones)


def per_device(tokens, cotangent, weight, momentum, gain, band):
    tokens, cotangent, momentum = tokens[0], cotangent[0], momentum[0]
    rep, shard = lax.axis_index("rep"), lax.axis_index("shard")
    z, core = rep // 4, rep % 2
    y, xh = shard // 2, shard % 2
    parity = (z % 2).astype(jnp.int32)

    def shard_at(dy, dx):
        return (((y + dy) % 4) * 2 + (xh ^ dx)).astype(jnp.int32)

    def step_shard(k, c):
        return jnp.where(c == 0, shard_at(STEPS[k][0], 0), shard_at(STEPS[k][1], 1))

    info = jnp.stack(
        [parity, core, rep % 4, *[step_shard(k, core) for k in range(4)], *[step_shard(k, 1 - core) for k in range(4)],
         *[shard_at(*a) for a in AWAY], 1 - parity]
    ).astype(jnp.int32)
    tables = [jnp.asarray(t) for t in dct_tables()]
    ones = jnp.asarray(np.kron(np.eye(4), np.ones((32, 32))).astype(np.float32), bf16)
    corner_positions = (jnp.arange(32)[:, None] * 64 + jnp.arange(32)[None, :]).reshape(1024, 1)
    mask = jnp.any(corner_positions == band[None, :], axis=1).astype(f32).reshape(32, 32)
    mask = jnp.tile(mask, (10, 4))

    def is_own(k, c):
        return c == 0 and STEPS[k][c] == 0

    def near_source(k):
        return lambda z, x, c, y: None if is_own(k, c) else (z, 3 - x if c else x, c, y + STEPS[k][c])

    def z_source(k):
        return lambda z, x, c, y: None if is_own(k, c) else (z - 1 if c else z + 1, x, c, y)

    def core_swap(value):
        return pull(value, lambda z, x, c, y: (z, x, 1 - c, y))

    own_half, = cut_columns(info, weight, [PARITY], HALF)
    first = [pull(own_half, near_source(k)) for k in range(4)]
    others, = cut_columns(info, tokens, [FAR + k for k in range(4)], ROWS, joined=True, after=(own_half,))
    others = core_swap(others)
    second = [pull(first[k], z_source(k)) for k in range(4)]
    cut = cut_columns(info, tokens, [AWAY_AT + k for k in range(4)], ROWS, True, after=(first[0],))
    cut += cut_columns(info, tokens, [AWAY_AT + k for k in range(4, 8)], ROWS, True, after=(second[0],))
    arrived = [pull(cut[k], from_shard(-dy, dx)) if k else cut[k] for k, (dy, dx) in enumerate(AWAY)]

    mine, theirs = project(info, tokens, others, weight, first, second, arrived[1:8])
    key_grad = key_gradient(info, mine, core_swap(theirs), cotangent, gain[None], [])

    keys = {(0, 1): pull(key_grad, from_shard(0, 1))}
    for dy in (1, 3, 2):
        keys[dy, 0] = pull(key_grad, from_shard(dy, 0))
    keys[1, 1] = pull(keys[0, 1], from_shard(1, 0))
    keys[3, 1] = pull(keys[0, 1], from_shard(3, 0))
    keys[2, 1] = pull(keys[2, 0], from_shard(0, 1))

    mine, theirs = token_gradient(
        info, key_grad, core_swap(key_grad), weight, first, second,
        [keys[a] for a in ((0, 1), (1, 0), (3, 0), (2, 0))],
    )
    input_grad = place_columns(info, mine, core_swap(theirs))

    keys[0, 0] = key_grad
    blended, corner, quarter, *parts = blend(
        info, arrived, [keys[(-dy) % 4, dx] for dy, dx in AWAY], momentum, mask, tables, input_grad
    )
    residue = remove_corner(blended, corner, tables)

    def group_source(k):
        return lambda z, x, c, y: (z, x ^ (k // 2), c ^ (k % 2), y)

    def pull_z(value, flip):
        return pull(value, lambda z, x, c, y: (z ^ flip, x, c, y)).astype(f32)

    parts = {k: pull(parts[k - 1], group_source(k)) for k in (2, 3, 1)}
    summed = add_parts(quarter, [parts[k] for k in (1, 2, 3)], residue)
    summed = (summed.astype(f32) + pull_z(summed, 1)).astype(bf16)
    p4, p2, p6 = (pull_z(summed, flip) for flip in (4, 2, 6))
    summed = ((summed.astype(f32) + p2) + (p4 + p6)).astype(bf16)
    quarters = [summed] + [pull(summed, group_source(k)) for k in (1, 2, 3)]
    update = normalized_update(info, quarters, tables, ones)
    return (input_grad[None], residue[None], update)


def solution(mesh):
    return jax.shard_map(
        per_device,
        mesh=mesh,
        in_specs=(
            P("rep", "shard", None),
            P("rep", "shard", None),
            P("shard", None),
            P("rep", "shard", None),
            P(),
            P(),
        ),
        out_specs=(P("rep", "shard", None), P("rep", "shard", None), P("shard", None)),
        check_vma=False,
    )
```

```python
import math

import jax
import jax.numpy as jnp
import numpy as np
from jax import lax
from jax.experimental import pallas as pl
from jax.experimental.pallas import tpu as pltpu
from jax.sharding import PartitionSpec as P

norm_epsilon = 1e-06
block_epsilon = 1e-06
decay_rate = 0.999
step_rate = 0.02

Z, XL, CORE, Y, XH = 8, 2, 2, 4, 2
X = XL * XH
TOK, D, KV, ROWS = 256, 5120, 1024, 640
HALF = KV // 2
bf16, f32 = jnp.bfloat16, jnp.float32
PARITY, IS_CORE1, ME, NEAR, FAR, AWAY_AT, OTHER_HALF = 0, 1, 2, 3, 7, 11, 19
AWAY = [(0, 0), (1, 0), (3, 0), (0, 1), (2, 0), (1, 1), (3, 1), (2, 1)]
STEPS = ((1, 0), (3, 1), (2, 3), (0, 2))
ANY = pl.BlockSpec(memory_space=pl.ANY)
VMEM = pl.BlockSpec(memory_space=pltpu.VMEM)
SMEM = pl.BlockSpec(memory_space=pltpu.SMEM)


def device_index(z, x, c, y):
    z, x, y = z % Z, x % X, y % Y
    return (((z * XL + x % XL) * CORE + c) * Y + y) * XH + x // XL


def pull(value, source):
    pairs = []
    for z in range(Z):
        for x in range(X):
            for c in range(CORE):
                for y in range(Y):
                    found = source(z, x, c, y)
                    if found is not None:
                        pairs.append((device_index(*found), device_index(z, x, c, y)))
    return lax.ppermute(value, ("rep", "shard"), pairs)


def from_shard(dy, dx):
    return lambda z, x, c, y: (z, x + 2 * dx, c, y + dy)


def split_bf16(table):
    high = table.astype(bf16)
    low = (table - high.astype(np.float32)).astype(bf16)
    return np.stack([high, low])


def dct_tables():
    freq = np.arange(64, dtype=np.float64)
    angle = math.pi * (2.0 * freq[None, :] + 1.0) * freq[:, None] / 128.0
    factor = np.where(freq[:, None] == 0.0, math.sqrt(1.0 / 64.0), math.sqrt(2.0 / 64.0))
    table = (factor * np.cos(angle))[:32].astype(np.float32)
    left = np.kron(np.eye(2, dtype=np.float32), table)
    right = np.kron(np.eye(4, dtype=np.float32), table.T)
    return split_bf16(left), split_bf16(right)


def split(value):
    high = value.astype(bf16)
    return high, (value - high.astype(f32)).astype(bf16)


def mm(a, b):
    return jnp.dot(a, b, preferred_element_type=f32)


def mm_left(table, value):
    high, low = split(value)
    return mm(table[0], high) + mm(table[0], low) + mm(table[1], high)


def mm_right(value, table):
    high, low = split(value)
    return mm(high, table[0]) + mm(low, table[0]) + mm(high, table[1])


def params(limit=56):
    return pltpu.CompilerParams(vmem_limit_bytes=limit * 1024 * 1024)


def cut_columns(info, value, slots, width, transposed=False, joined=False, after=()):
    rows, count = value.shape[0], len(slots)

    def kernel(info_ref, *refs):
        for k in range(count):
            block = refs[k][...]
            block = block.T if transposed else block
            if joined:
                refs[-1][:, width * k : width * k + width] = block
            else:
                refs[count + len(after) + k][...] = block

    shape = (rows, width * count) if joined else (width, rows) if transposed else (rows, width)
    outs = 1 if joined else count
    return pl.pallas_call(
        kernel,
        grid_spec=pltpu.PrefetchScalarGridSpec(
            num_scalar_prefetch=1,
            grid=(1,),
            in_specs=[pl.BlockSpec((rows, width), lambda i, s, k=k: (0, s[k])) for k in slots] + [ANY] * len(after),
            out_specs=[pl.BlockSpec(shape, lambda i, s: (0, 0))] * outs,
        ),
        out_shape=[jax.ShapeDtypeStruct(shape, value.dtype)] * outs,
        compiler_params=params(),
        cost_estimate=pl.CostEstimate(flops=0, bytes_accessed=4 * rows * width * count, transcendentals=0),
    )(info, *([value] * count), *after)


def column_half(ref, p):
    return ref[:, pl.ds(pl.multiple_of(p * HALF, HALF), HALF)]


def project(info, tokens, others, own, first, second, after):
    def kernel(info_ref, t_ref, o_ref, own_ref, *refs):
        ws, outs = refs[:8], refs[8 + len(after) : 10 + len(after)]
        toks, other, weights, sems = refs[10 + len(after) :]
        p, core = info_ref[PARITY], info_ref[IS_CORE1]
        copies = []

        def start(source, target):
            copies.append(pltpu.make_async_copy(source, target, sems.at[len(copies)]))
            copies[-1].start()

        start(o_ref, other)
        for k in range(4):
            at = pl.ds(pl.multiple_of(info_ref[NEAR + k] * ROWS, 128), ROWS)
            start(t_ref.at[:, at], toks.at[k])
        for k in range(4):
            for h in range(2):
                start(ws[4 * h + k], weights.at[2 * k + h])
        for copy in copies[:5]:
            copy.wait()
        sums = [[None, None], [None, None]]
        for k in range(4):
            for h in range(2):
                copies[5 + 2 * k + h].wait()
                w = weights[2 * k + h]
                if k == 3:
                    w = jnp.where(core == 0, column_half(own_ref, p if h == 0 else 1 - p), w)
                for n, t in enumerate((toks[k], other[:, ROWS * k : ROWS * k + ROWS])):
                    term = mm(t, w)
                    sums[n][h] = term if k == 0 else sums[n][h] + term
        for n in range(2):
            for h in range(2):
                outs[n][:, HALF * h : HALF * h + HALF] = sums[n][h]

    return pl.pallas_call(
        kernel,
        in_specs=[SMEM, ANY, ANY, VMEM] + [ANY] * (8 + len(after)),
        out_specs=[VMEM] * 2,
        out_shape=[jax.ShapeDtypeStruct((TOK, KV), f32)] * 2,
        scratch_shapes=[
            pltpu.VMEM((4, TOK, ROWS), bf16),
            pltpu.VMEM((TOK, 4 * ROWS), bf16),
            pltpu.VMEM((8, ROWS, HALF), bf16),
            pltpu.SemaphoreType.DMA((13,)),
        ],
        compiler_params=params(),
        cost_estimate=pl.CostEstimate(flops=2 * TOK * D * KV, bytes_accessed=(KV * D + TOK * D) * 2, transcendentals=0),
    )(info, tokens, others, own, *first, *second, *after)


def key_gradient(info, mine, arrived, cotangent, gain, after):
    def kernel(s_ref, m_ref, r_ref, ca_ref, cb_ref, ga_ref, gb_ref, *refs):
        out_ref = refs[-1]
        p = s_ref[PARITY]
        both = m_ref[...] + r_ref[...]
        a, b = both[:, :HALF], both[:, HALF:]
        sa = ca_ref[...].astype(f32) * ga_ref[...]
        sb = cb_ref[...].astype(f32) * gb_ref[...]
        square = jnp.sum(a * a, axis=-1, keepdims=True) + jnp.sum(b * b, axis=-1, keepdims=True)
        cross = jnp.sum(sa * a, axis=-1, keepdims=True) + jnp.sum(sb * b, axis=-1, keepdims=True)
        inverse = lax.rsqrt(square * (1.0 / KV) + norm_epsilon)
        factor = inverse * inverse * (cross * (1.0 / KV))
        out_ref[:, pl.ds(pl.multiple_of(p * HALF, HALF), HALF)] = (inverse * (sa - a * factor)).astype(bf16)
        out_ref[:, pl.ds(pl.multiple_of((1 - p) * HALF, HALF), HALF)] = (inverse * (sb - b * factor)).astype(bf16)

    full = pl.BlockSpec((TOK, KV), lambda i, s: (0, 0))
    return pl.pallas_call(
        kernel,
        grid_spec=pltpu.PrefetchScalarGridSpec(
            num_scalar_prefetch=1,
            grid=(1,),
            in_specs=[
                full,
                full,
                pl.BlockSpec((TOK, HALF), lambda i, s: (0, s[PARITY])),
                pl.BlockSpec((TOK, HALF), lambda i, s: (0, 1 - s[PARITY])),
                pl.BlockSpec((1, HALF), lambda i, s: (0, s[PARITY])),
                pl.BlockSpec((1, HALF), lambda i, s: (0, 1 - s[PARITY])),
            ]
            + [ANY] * len(after),
            out_specs=full,
        ),
        out_shape=jax.ShapeDtypeStruct((TOK, KV), bf16),
        compiler_params=params(32),
        cost_estimate=pl.CostEstimate(flops=10 * TOK * KV, bytes_accessed=TOK * KV * 12, transcendentals=TOK),
    )(info, mine, arrived, cotangent, cotangent, gain, gain, *after)


def token_gradient(info, key_grad, other_keys, own, first, second, after):
    def kernel(info_ref, k_ref, o_ref, own_ref, *refs):
        ws, outs = refs[:8], refs[8 + len(after) :]
        p, core = info_ref[PARITY], info_ref[IS_CORE1]
        for k in range(4):
            wa, wb = ws[k][...], ws[4 + k][...]
            if k == 3:
                wa = jnp.where(core == 0, column_half(own_ref, p), wa)
                wb = jnp.where(core == 0, column_half(own_ref, 1 - p), wb)
            for keys, out in zip((k_ref, o_ref), outs):
                value = against(column_half(keys, p), wa) + against(column_half(keys, 1 - p), wb)
                out[:, ROWS * k : ROWS * k + ROWS] = value.astype(bf16)

    return pl.pallas_call(
        kernel,
        in_specs=[SMEM] + [VMEM] * 11 + [ANY] * len(after),
        out_specs=[VMEM] * 2,
        out_shape=[jax.ShapeDtypeStruct((TOK, 4 * ROWS), bf16)] * 2,
        compiler_params=params(),
        cost_estimate=pl.CostEstimate(flops=2 * TOK * KV * D, bytes_accessed=(KV * D + TOK * D) * 2, transcendentals=0),
    )(info, key_grad, other_keys, own, *first, *second, *after)


def place_columns(info, mine, arrived):
    def kernel(info_ref, m_ref, r_ref, out_ref):
        for slot, ref in ((NEAR, m_ref), (FAR, r_ref)):
            for k in range(4):
                at = pl.ds(pl.multiple_of(info_ref[slot + k] * ROWS, 128), ROWS)
                out_ref[:, at] = ref[:, ROWS * k : ROWS * k + ROWS]

    return pl.pallas_call(
        kernel,
        in_specs=[SMEM] + [VMEM] * 2,
        out_specs=VMEM,
        out_shape=jax.ShapeDtypeStruct((TOK, D), bf16),
        compiler_params=params(),
        cost_estimate=pl.CostEstimate(flops=0, bytes_accessed=4 * TOK * D, transcendentals=0),
    )(info, mine, arrived)


def against(a, b):
    return lax.dot_general(a, b, (((1,), (1,)), ((), ())), preferred_element_type=f32)


def across(a, b):
    return lax.dot_general(a, b, (((0,), (0,)), ((), ())), preferred_element_type=f32)


def to_corner(value, left, right):
    narrow = mm_right(value, right)
    return jnp.concatenate([mm_left(left, narrow[128 * i : 128 * i + 128]) for i in range(5)], axis=0)


def from_corner(corner, left, right):
    high, low = split(corner)
    blocks = []
    for i in range(5):
        h, l = high[64 * i : 64 * i + 64], low[64 * i : 64 * i + 64]
        blocks.append(across(left[0], h) + across(left[0], l) + across(left[1], h))
    high, low = split(jnp.concatenate(blocks, axis=0))
    return against(high, right[0]) + against(low, right[0]) + against(high, right[1])


def blend(info, tokens, keys, momentum, mask, tables, after):
    count = len(keys)
    width = 256

    def kernel(info_ref, *refs):
        toks, ks = refs[:count], refs[count : 2 * count]
        momentum_ref, mask_ref, left_ref, right_ref, _, blended_ref, corner_ref, *parts = refs[2 * count :]
        t = jnp.concatenate([ref[...] for ref in toks], axis=1)
        k = jnp.concatenate([ref[...] for ref in ks], axis=0)
        blended = decay_rate * momentum_ref[...] + step_rate * mm(t, k)
        blended_ref[...] = blended
        corner = to_corner(blended, left_ref[...], right_ref[...]) * mask_ref[...]
        corner_ref[0] = corner
        for i in range(4):

            @pl.when(pl.program_id(0) == i)
            def _():
                parts[i][...] = corner.astype(parts[i].dtype)

    def whole(a):
        return pl.BlockSpec(a.shape, lambda i, s: (0,) * a.ndim)

    columns = pl.BlockSpec((ROWS, width), lambda i, s: (0, s[ME] ^ i))
    specs = [pl.BlockSpec((ROWS, TOK), lambda i, s: (0, 0))] * count
    specs += [pl.BlockSpec((TOK, width), lambda i, s: (0, s[ME] ^ i))] * count
    specs += [columns, whole(mask), whole(tables[0]), whole(tables[1]), ANY]
    part = pl.BlockSpec((320, 128), lambda i, s: (0, 0))
    return pl.pallas_call(
        kernel,
        grid_spec=pltpu.PrefetchScalarGridSpec(
            num_scalar_prefetch=1,
            grid=(KV // width,),
            in_specs=specs,
            out_specs=[columns, pl.BlockSpec((1, 320, 128), lambda i, s: (s[ME] ^ i, 0, 0))] + [part] * 4,
        ),
        out_shape=[jax.ShapeDtypeStruct((ROWS, KV), f32), jax.ShapeDtypeStruct((4, 320, 128), f32)]
        + [jax.ShapeDtypeStruct((320, 128), t) for t in (f32, bf16, bf16, bf16)],
        compiler_params=params(),
        cost_estimate=pl.CostEstimate(
            flops=2 * TOK * count * KV * ROWS, bytes_accessed=ROWS * KV * 8 + count * TOK * (ROWS + KV) * 2, transcendentals=0
        ),
    )(info, *tokens, *keys, momentum, mask, *tables, after)


def remove_corner(blended, corner, tables):
    def kernel(blended_ref, corner_ref, left_ref, right_ref, out_ref):
        out_ref[...] = blended_ref[...] - from_corner(corner_ref[0], left_ref[...], right_ref[...])

    return pl.pallas_call(
        kernel,
        grid=(4,),
        in_specs=[
            pl.BlockSpec((ROWS, 256), lambda i: (0, i)),
            pl.BlockSpec((1, 320, 128), lambda i: (i, 0, 0)),
            pl.BlockSpec(tables[0].shape, lambda i: (0, 0, 0)),
            pl.BlockSpec(tables[1].shape, lambda i: (0, 0, 0)),
        ],
        out_specs=pl.BlockSpec((ROWS, 256), lambda i: (0, i)),
        out_shape=jax.ShapeDtypeStruct((ROWS, KV), f32),
        compiler_params=params(),
        cost_estimate=pl.CostEstimate(flops=2 * ROWS * KV * 256, bytes_accessed=ROWS * KV * 8, transcendentals=0),
    )(blended, corner, *tables)


def add_parts(own, parts, after):
    def kernel(a, b, c, d, _, out_ref):
        out_ref[...] = (a[...] + b[...].astype(f32) + (c[...].astype(f32) + d[...].astype(f32))).astype(bf16)

    return pl.pallas_call(
        kernel,
        in_specs=[VMEM] * 4 + [ANY],
        out_specs=VMEM,
        out_shape=jax.ShapeDtypeStruct(own.shape, bf16),
        compiler_params=params(),
    )(own, *parts, after)


def normalized_update(info, quarters, tables, ones, after):
    def kernel(info_ref, a, b, c, d, left_ref, right_ref, ones_ref, _, out_ref):
        for k, ref in enumerate((a, b, c, d)):
            corner = ref[...].astype(f32)
            energy = jnp.sum((corner * corner).reshape(10, 32, 128), axis=1)
            high, low = split(energy)
            energy = mm(high, ones_ref[...]) + mm(low, ones_ref[...])
            scale = lax.rsqrt(energy * (1.0 / 4096.0) + block_epsilon)
            corner = (corner.reshape(10, 32, 128) * scale[:, None, :]).reshape(320, 128)
            columns = pl.ds(pl.multiple_of((info_ref[ME] ^ k) * 256, 256), 256)
            out_ref[:, columns] = from_corner(corner, left_ref[...], right_ref[...]).astype(bf16)

    return pl.pallas_call(
        kernel,
        in_specs=[SMEM] + [VMEM] * 7 + [ANY],
        out_specs=VMEM,
        out_shape=jax.ShapeDtypeStruct((ROWS, KV), bf16),
        compiler_params=params(),
    )(info, *quarters, *tables, ones, after)


def per_device(tokens, cotangent, weight, momentum, gain, band):
    tokens, cotangent, momentum = tokens[0], cotangent[0], momentum[0]
    rep, shard = lax.axis_index("rep"), lax.axis_index("shard")
    z, core = rep // 4, rep % 2
    y, xh = shard // 2, shard % 2
    parity = (z % 2).astype(jnp.int32)

    def shard_at(dy, dx):
        return (((y + dy) % 4) * 2 + (xh ^ dx)).astype(jnp.int32)

    def step_shard(k, c):
        return jnp.where(c == 0, shard_at(STEPS[k][0], 0), shard_at(STEPS[k][1], 1))

    info = jnp.stack(
        [parity, core, rep % 4, *[step_shard(k, core) for k in range(4)], *[step_shard(k, 1 - core) for k in range(4)],
         *[shard_at(*a) for a in AWAY], 1 - parity]
    ).astype(jnp.int32)
    tables = [jnp.asarray(t) for t in dct_tables()]
    ones = jnp.asarray(np.kron(np.eye(4), np.ones((32, 32))).astype(np.float32), bf16)
    corner_positions = (jnp.arange(32)[:, None] * 64 + jnp.arange(32)[None, :]).reshape(1024, 1)
    mask = jnp.any(corner_positions == band[None, :], axis=1).astype(f32).reshape(32, 32)
    mask = jnp.tile(mask, (10, 4))

    def is_own(k, c):
        return c == 0 and STEPS[k][c] == 0

    def near_source(k):
        return lambda z, x, c, y: None if is_own(k, c) else (z, 3 - x if c else x, c, y + STEPS[k][c])

    def z_source(k):
        return lambda z, x, c, y: None if is_own(k, c) else (z - 1 if c else z + 1, x, c, y)

    def core_swap(value):
        return pull(value, lambda z, x, c, y: (z, x, 1 - c, y))

    own_half, = cut_columns(info, weight, [PARITY], HALF)
    first = [pull(own_half, near_source(k)) for k in range(4)]
    others, = cut_columns(info, tokens, [FAR + k for k in range(4)], ROWS, joined=True, after=(own_half,))
    others = core_swap(others)
    second = [pull(first[k], z_source(k)) for k in range(4)]
    cut = cut_columns(info, tokens, [AWAY_AT + k for k in range(4)], ROWS, True, after=(first[0],))
    cut += cut_columns(info, tokens, [AWAY_AT + k for k in range(4, 8)], ROWS, True, after=(second[0],))
    arrived = [pull(cut[k], from_shard(-dy, dx)) if k else cut[k] for k, (dy, dx) in enumerate(AWAY)]

    mine, theirs = project(info, tokens, others, weight, first, second, arrived[1:8])
    key_grad = key_gradient(info, mine, core_swap(theirs), cotangent, gain[None], [])

    keys = {(0, 1): pull(key_grad, from_shard(0, 1))}
    for dy in (1, 3, 2):
        keys[dy, 0] = pull(key_grad, from_shard(dy, 0))
    keys[1, 1] = pull(keys[0, 1], from_shard(1, 0))
    keys[3, 1] = pull(keys[0, 1], from_shard(3, 0))
    keys[2, 1] = pull(keys[2, 0], from_shard(0, 1))

    mine, theirs = token_gradient(
        info, key_grad, core_swap(key_grad), weight, first, second,
        [keys[a] for a in ((0, 1), (1, 0), (3, 0), (2, 0))],
    )
    input_grad = place_columns(info, mine, core_swap(theirs))

    keys[0, 0] = key_grad
    blended, corner, quarter, *parts = blend(
        info, arrived, [keys[(-dy) % 4, dx] for dy, dx in AWAY], momentum, mask, tables, mine
    )
    residue = remove_corner(blended, corner, tables)

    def group_source(k):
        return lambda z, x, c, y: (z, x ^ (k // 2), c ^ (k % 2), y)

    def pull_z(value, flip):
        return pull(value, lambda z, x, c, y: (z ^ flip, x, c, y)).astype(f32)

    parts = {k: pull(parts[k - 1], group_source(k)) for k in (2, 3, 1)}
    summed = add_parts(quarter, [parts[k] for k in (1, 2, 3)], residue)
    summed = (summed.astype(f32) + pull_z(summed, 1)).astype(bf16)
    p4, p2, p6 = (pull_z(summed, flip) for flip in (4, 2, 6))
    summed = ((summed.astype(f32) + p2) + (p4 + p6)).astype(bf16)
    quarters = [summed] + [pull(summed, group_source(k)) for k in (1, 2, 3)]
    update = normalized_update(info, quarters, tables, ones, input_grad)
    return (input_grad[None], residue[None], update)


def solution(mesh):
    return jax.shard_map(
        per_device,
        mesh=mesh,
        in_specs=(
            P("rep", "shard", None),
            P("rep", "shard", None),
            P("shard", None),
            P("rep", "shard", None),
            P(),
            P(),
        ),
        out_specs=(P("rep", "shard", None), P("rep", "shard", None), P("shard", None)),
        check_vma=False,
    )
```

```python
import math

import jax
import jax.numpy as jnp
import numpy as np
from jax import lax
from jax.experimental import pallas as pl
from jax.experimental.pallas import tpu as pltpu
from jax.sharding import PartitionSpec as P

norm_epsilon = 1e-06
block_epsilon = 1e-06
decay_rate = 0.999
step_rate = 0.02

Z, XL, CORE, Y, XH = 8, 2, 2, 4, 2
X = XL * XH
TOK, D, KV, ROWS = 256, 5120, 1024, 640
HALF = KV // 2
bf16, f32 = jnp.bfloat16, jnp.float32
PARITY, IS_CORE1, ME, NEAR, FAR, AWAY_AT, OTHER_HALF = 0, 1, 2, 3, 7, 11, 19
AWAY = [(0, 0), (1, 0), (3, 0), (0, 1), (2, 0), (1, 1), (3, 1), (2, 1)]
STEPS = ((1, 0), (3, 1), (2, 3), (0, 2))
ANY = pl.BlockSpec(memory_space=pl.ANY)
VMEM = pl.BlockSpec(memory_space=pltpu.VMEM)
SMEM = pl.BlockSpec(memory_space=pltpu.SMEM)


def device_index(z, x, c, y):
    z, x, y = z % Z, x % X, y % Y
    return (((z * XL + x % XL) * CORE + c) * Y + y) * XH + x // XL


def pull(value, source):
    pairs = []
    for z in range(Z):
        for x in range(X):
            for c in range(CORE):
                for y in range(Y):
                    found = source(z, x, c, y)
                    if found is not None:
                        pairs.append((device_index(*found), device_index(z, x, c, y)))
    return lax.ppermute(value, ("rep", "shard"), pairs)


def from_shard(dy, dx):
    return lambda z, x, c, y: (z, x + 2 * dx, c, y + dy)


def split_bf16(table):
    high = table.astype(bf16)
    low = (table - high.astype(np.float32)).astype(bf16)
    return np.stack([high, low])


def dct_tables():
    freq = np.arange(64, dtype=np.float64)
    angle = math.pi * (2.0 * freq[None, :] + 1.0) * freq[:, None] / 128.0
    factor = np.where(freq[:, None] == 0.0, math.sqrt(1.0 / 64.0), math.sqrt(2.0 / 64.0))
    table = (factor * np.cos(angle))[:32].astype(np.float32)
    left = np.kron(np.eye(2, dtype=np.float32), table)
    right = np.kron(np.eye(4, dtype=np.float32), table.T)
    return split_bf16(left), split_bf16(right)


def split(value):
    high = value.astype(bf16)
    return high, (value - high.astype(f32)).astype(bf16)


def mm(a, b):
    return jnp.dot(a, b, preferred_element_type=f32)


def mm_left(table, value):
    high, low = split(value)
    return mm(jnp.concatenate([table[0], table[0], table[1]], axis=1), jnp.concatenate([high, low, high], axis=0))


def mm_right(value, table):
    high, low = split(value)
    return mm(jnp.concatenate([high, low, high], axis=1), jnp.concatenate([table[0], table[0], table[1]], axis=0))


def params(limit=56):
    return pltpu.CompilerParams(vmem_limit_bytes=limit * 1024 * 1024)


def cut_columns(info, value, slots, width, transposed=False, joined=False, after=()):
    rows, count = value.shape[0], len(slots)

    def kernel(info_ref, *refs):
        for k in range(count):
            block = refs[k][...]
            block = block.T if transposed else block
            if joined:
                refs[-1][:, width * k : width * k + width] = block
            else:
                refs[count + len(after) + k][...] = block

    shape = (rows, width * count) if joined else (width, rows) if transposed else (rows, width)
    outs = 1 if joined else count
    return pl.pallas_call(
        kernel,
        grid_spec=pltpu.PrefetchScalarGridSpec(
            num_scalar_prefetch=1,
            grid=(1,),
            in_specs=[pl.BlockSpec((rows, width), lambda i, s, k=k: (0, s[k])) for k in slots] + [ANY] * len(after),
            out_specs=[pl.BlockSpec(shape, lambda i, s: (0, 0))] * outs,
        ),
        out_shape=[jax.ShapeDtypeStruct(shape, value.dtype)] * outs,
        compiler_params=params(),
        cost_estimate=pl.CostEstimate(flops=0, bytes_accessed=4 * rows * width * count, transcendentals=0),
    )(info, *([value] * count), *after)


def column_half(ref, p):
    return ref[:, pl.ds(pl.multiple_of(p * HALF, HALF), HALF)]


def project(info, tokens, others, own, first, second, after):
    def kernel(info_ref, t_ref, o_ref, own_ref, *refs):
        ws, outs = refs[:8], refs[8 + len(after) : 10 + len(after)]
        toks, other, weights, sems = refs[10 + len(after) :]
        p, core = info_ref[PARITY], info_ref[IS_CORE1]
        copies = []

        def start(source, target):
            copies.append(pltpu.make_async_copy(source, target, sems.at[len(copies)]))
            copies[-1].start()

        start(o_ref, other)
        for k in range(4):
            at = pl.ds(pl.multiple_of(info_ref[NEAR + k] * ROWS, 128), ROWS)
            start(t_ref.at[:, at], toks.at[k])
        for k in range(4):
            for h in range(2):
                start(ws[4 * h + k], weights.at[2 * k + h])
        for copy in copies[:5]:
            copy.wait()
        sums = [[None, None], [None, None]]
        for k in range(4):
            for h in range(2):
                copies[5 + 2 * k + h].wait()
                w = weights[2 * k + h]
                if k == 3:
                    w = jnp.where(core == 0, column_half(own_ref, p if h == 0 else 1 - p), w)
                for n, t in enumerate((toks[k], other[:, ROWS * k : ROWS * k + ROWS])):
                    term = mm(t, w)
                    sums[n][h] = term if k == 0 else sums[n][h] + term
        for n in range(2):
            for h in range(2):
                outs[n][:, HALF * h : HALF * h + HALF] = sums[n][h].astype(outs[n].dtype)

    return pl.pallas_call(
        kernel,
        in_specs=[SMEM, ANY, ANY, VMEM] + [ANY] * (8 + len(after)),
        out_specs=[VMEM] * 2,
        out_shape=[jax.ShapeDtypeStruct((TOK, KV), t) for t in (f32, bf16)],
        scratch_shapes=[
            pltpu.VMEM((4, TOK, ROWS), bf16),
            pltpu.VMEM((TOK, 4 * ROWS), bf16),
            pltpu.VMEM((8, ROWS, HALF), bf16),
            pltpu.SemaphoreType.DMA((13,)),
        ],
        compiler_params=params(),
        cost_estimate=pl.CostEstimate(flops=2 * TOK * D * KV, bytes_accessed=(KV * D + TOK * D) * 2, transcendentals=0),
    )(info, tokens, others, own, *first, *second, *after)


def key_gradient(info, mine, arrived, cotangent, gain, after):
    def kernel(s_ref, m_ref, r_ref, ca_ref, cb_ref, ga_ref, gb_ref, *refs):
        out_ref = refs[-1]
        p = s_ref[PARITY]
        both = m_ref[...] + r_ref[...].astype(f32)
        a, b = both[:, :HALF], both[:, HALF:]
        sa = ca_ref[...].astype(f32) * ga_ref[...]
        sb = cb_ref[...].astype(f32) * gb_ref[...]
        square = jnp.sum(a * a, axis=-1, keepdims=True) + jnp.sum(b * b, axis=-1, keepdims=True)
        cross = jnp.sum(sa * a, axis=-1, keepdims=True) + jnp.sum(sb * b, axis=-1, keepdims=True)
        inverse = lax.rsqrt(square * (1.0 / KV) + norm_epsilon)
        factor = inverse * inverse * (cross * (1.0 / KV))
        out_ref[:, pl.ds(pl.multiple_of(p * HALF, HALF), HALF)] = (inverse * (sa - a * factor)).astype(bf16)
        out_ref[:, pl.ds(pl.multiple_of((1 - p) * HALF, HALF), HALF)] = (inverse * (sb - b * factor)).astype(bf16)

    full = pl.BlockSpec((TOK, KV), lambda i, s: (0, 0))
    return pl.pallas_call(
        kernel,
        grid_spec=pltpu.PrefetchScalarGridSpec(
            num_scalar_prefetch=1,
            grid=(1,),
            in_specs=[
                full,
                full,
                pl.BlockSpec((TOK, HALF), lambda i, s: (0, s[PARITY])),
                pl.BlockSpec((TOK, HALF), lambda i, s: (0, 1 - s[PARITY])),
                pl.BlockSpec((1, HALF), lambda i, s: (0, s[PARITY])),
                pl.BlockSpec((1, HALF), lambda i, s: (0, 1 - s[PARITY])),
            ]
            + [ANY] * len(after),
            out_specs=full,
        ),
        out_shape=jax.ShapeDtypeStruct((TOK, KV), bf16),
        compiler_params=params(32),
        cost_estimate=pl.CostEstimate(flops=10 * TOK * KV, bytes_accessed=TOK * KV * 12, transcendentals=TOK),
    )(info, mine, arrived, cotangent, cotangent, gain, gain, *after)


def token_gradient(info, key_grad, other_keys, own, first, second, after):
    def kernel(info_ref, k_ref, o_ref, own_ref, *refs):
        ws, outs = refs[:8], refs[8 + len(after) :]
        p, core = info_ref[PARITY], info_ref[IS_CORE1]
        for k in range(4):
            wa, wb = ws[k][...], ws[4 + k][...]
            if k == 3:
                wa = jnp.where(core == 0, column_half(own_ref, p), wa)
                wb = jnp.where(core == 0, column_half(own_ref, 1 - p), wb)
            for keys, out in zip((k_ref, o_ref), outs):
                value = against(column_half(keys, p), wa) + against(column_half(keys, 1 - p), wb)
                out[:, ROWS * k : ROWS * k + ROWS] = value.astype(bf16)

    return pl.pallas_call(
        kernel,
        in_specs=[SMEM] + [VMEM] * 11 + [ANY] * len(after),
        out_specs=[VMEM] * 2,
        out_shape=[jax.ShapeDtypeStruct((TOK, 4 * ROWS), bf16)] * 2,
        compiler_params=params(),
        cost_estimate=pl.CostEstimate(flops=2 * TOK * KV * D, bytes_accessed=(KV * D + TOK * D) * 2, transcendentals=0),
    )(info, key_grad, other_keys, own, *first, *second, *after)


def place_columns(info, mine, arrived):
    def kernel(info_ref, m_ref, r_ref, out_ref):
        for slot, ref in ((NEAR, m_ref), (FAR, r_ref)):
            for k in range(4):
                at = pl.ds(pl.multiple_of(info_ref[slot + k] * ROWS, 128), ROWS)
                out_ref[:, at] = ref[:, ROWS * k : ROWS * k + ROWS]

    return pl.pallas_call(
        kernel,
        in_specs=[SMEM] + [VMEM] * 2,
        out_specs=VMEM,
        out_shape=jax.ShapeDtypeStruct((TOK, D), bf16),
        compiler_params=params(),
        cost_estimate=pl.CostEstimate(flops=0, bytes_accessed=4 * TOK * D, transcendentals=0),
    )(info, mine, arrived)


def against(a, b):
    return lax.dot_general(a, b, (((1,), (1,)), ((), ())), preferred_element_type=f32)


def across(a, b):
    return lax.dot_general(a, b, (((0,), (0,)), ((), ())), preferred_element_type=f32)


def to_corner(value, left, right):
    narrow = mm_right(value, right)
    return jnp.concatenate([mm_left(left, narrow[128 * i : 128 * i + 128]) for i in range(5)], axis=0)


def from_corner(corner, left, right):
    high, low = split(corner)
    blocks = []
    for i in range(5):
        h, l = high[64 * i : 64 * i + 64], low[64 * i : 64 * i + 64]
        blocks.append(across(left[0], h) + across(left[0], l) + across(left[1], h))
    high, low = split(jnp.concatenate(blocks, axis=0))
    return against(high, right[0]) + against(low, right[0]) + against(high, right[1])


def blend(info, tokens, keys, momentum, mask, tables, after):
    count = len(keys)
    width = 256

    def kernel(info_ref, *refs):
        toks, ks = refs[:count], refs[count : 2 * count]
        momentum_ref, mask_ref, left_ref, right_ref, _, blended_ref, corner_ref, *parts = refs[2 * count :]
        t = jnp.concatenate([ref[...] for ref in toks], axis=1)
        k = jnp.concatenate([ref[...] for ref in ks], axis=0)
        blended = decay_rate * momentum_ref[...] + step_rate * mm(t, k)
        blended_ref[...] = blended
        corner = to_corner(blended, left_ref[...], right_ref[...]) * mask_ref[...]
        corner_ref[0] = corner
        for i in range(4):

            @pl.when(pl.program_id(0) == i)
            def _():
                parts[i][...] = corner.astype(parts[i].dtype)

    def whole(a):
        return pl.BlockSpec(a.shape, lambda i, s: (0,) * a.ndim)

    columns = pl.BlockSpec((ROWS, width), lambda i, s: (0, s[ME] ^ i))
    specs = [pl.BlockSpec((ROWS, TOK), lambda i, s: (0, 0))] * count
    specs += [pl.BlockSpec((TOK, width), lambda i, s: (0, s[ME] ^ i))] * count
    specs += [columns, whole(mask), whole(tables[0]), whole(tables[1]), ANY]
    part = pl.BlockSpec((320, 128), lambda i, s: (0, 0))
    return pl.pallas_call(
        kernel,
        grid_spec=pltpu.PrefetchScalarGridSpec(
            num_scalar_prefetch=1,
            grid=(KV // width,),
            in_specs=specs,
            out_specs=[columns, pl.BlockSpec((1, 320, 128), lambda i, s: (s[ME] ^ i, 0, 0))] + [part] * 4,
        ),
        out_shape=[jax.ShapeDtypeStruct((ROWS, KV), f32), jax.ShapeDtypeStruct((4, 320, 128), f32)]
        + [jax.ShapeDtypeStruct((320, 128), t) for t in (f32, bf16, bf16, bf16)],
        compiler_params=params(),
        cost_estimate=pl.CostEstimate(
            flops=2 * TOK * count * KV * ROWS, bytes_accessed=ROWS * KV * 8 + count * TOK * (ROWS + KV) * 2, transcendentals=0
        ),
    )(info, *tokens, *keys, momentum, mask, *tables, after)


def remove_corner(blended, corner, tables):
    def kernel(blended_ref, corner_ref, left_ref, right_ref, out_ref):
        out_ref[...] = blended_ref[...] - from_corner(corner_ref[0], left_ref[...], right_ref[...])

    return pl.pallas_call(
        kernel,
        grid=(4,),
        in_specs=[
            pl.BlockSpec((ROWS, 256), lambda i: (0, i)),
            pl.BlockSpec((1, 320, 128), lambda i: (i, 0, 0)),
            pl.BlockSpec(tables[0].shape, lambda i: (0, 0, 0)),
            pl.BlockSpec(tables[1].shape, lambda i: (0, 0, 0)),
        ],
        out_specs=pl.BlockSpec((ROWS, 256), lambda i: (0, i)),
        out_shape=jax.ShapeDtypeStruct((ROWS, KV), f32),
        compiler_params=params(),
        cost_estimate=pl.CostEstimate(flops=2 * ROWS * KV * 256, bytes_accessed=ROWS * KV * 8, transcendentals=0),
    )(blended, corner, *tables)


def add_parts(own, parts, after):
    def kernel(a, b, c, d, _, out_ref):
        out_ref[...] = (a[...] + b[...].astype(f32) + (c[...].astype(f32) + d[...].astype(f32))).astype(bf16)

    return pl.pallas_call(
        kernel,
        in_specs=[VMEM] * 4 + [ANY],
        out_specs=VMEM,
        out_shape=jax.ShapeDtypeStruct(own.shape, bf16),
        compiler_params=params(),
    )(own, *parts, after)


def normalized_update(info, quarters, tables, ones, after):
    def kernel(info_ref, a, b, c, d, left_ref, right_ref, ones_ref, _, out_ref):
        for k, ref in enumerate((a, b, c, d)):
            corner = ref[...].astype(f32)
            energy = jnp.sum((corner * corner).reshape(10, 32, 128), axis=1)
            high, low = split(energy)
            energy = mm(high, ones_ref[...]) + mm(low, ones_ref[...])
            scale = lax.rsqrt(energy * (1.0 / 4096.0) + block_epsilon)
            corner = (corner.reshape(10, 32, 128) * scale[:, None, :]).reshape(320, 128)
            columns = pl.ds(pl.multiple_of((info_ref[ME] ^ k) * 256, 256), 256)
            out_ref[:, columns] = from_corner(corner, left_ref[...], right_ref[...]).astype(bf16)

    return pl.pallas_call(
        kernel,
        in_specs=[SMEM] + [VMEM] * 7 + [ANY],
        out_specs=VMEM,
        out_shape=jax.ShapeDtypeStruct((ROWS, KV), bf16),
        compiler_params=params(),
    )(info, *quarters, *tables, ones, after)


def per_device(tokens, cotangent, weight, momentum, gain, band):
    tokens, cotangent, momentum = tokens[0], cotangent[0], momentum[0]
    rep, shard = lax.axis_index("rep"), lax.axis_index("shard")
    z, core = rep // 4, rep % 2
    y, xh = shard // 2, shard % 2
    parity = (z % 2).astype(jnp.int32)

    def shard_at(dy, dx):
        return (((y + dy) % 4) * 2 + (xh ^ dx)).astype(jnp.int32)

    def step_shard(k, c):
        return jnp.where(c == 0, shard_at(STEPS[k][0], 0), shard_at(STEPS[k][1], 1))

    info = jnp.stack(
        [parity, core, rep % 4, *[step_shard(k, core) for k in range(4)], *[step_shard(k, 1 - core) for k in range(4)],
         *[shard_at(*a) for a in AWAY], 1 - parity]
    ).astype(jnp.int32)
    tables = [jnp.asarray(t) for t in dct_tables()]
    ones = jnp.asarray(np.kron(np.eye(4), np.ones((32, 32))).astype(np.float32), bf16)
    corner_positions = (jnp.arange(32)[:, None] * 64 + jnp.arange(32)[None, :]).reshape(1024, 1)
    mask = jnp.any(corner_positions == band[None, :], axis=1).astype(f32).reshape(32, 32)
    mask = jnp.tile(mask, (10, 4))

    def is_own(k, c):
        return c == 0 and STEPS[k][c] == 0

    def near_source(k):
        return lambda z, x, c, y: None if is_own(k, c) else (z, 3 - x if c else x, c, y + STEPS[k][c])

    def z_source(k):
        return lambda z, x, c, y: None if is_own(k, c) else (z - 1 if c else z + 1, x, c, y)

    def core_swap(value):
        return pull(value, lambda z, x, c, y: (z, x, 1 - c, y))

    own_half, = cut_columns(info, weight, [PARITY], HALF)
    first = [pull(own_half, near_source(k)) for k in range(4)]
    others, = cut_columns(info, tokens, [FAR + k for k in range(4)], ROWS, joined=True, after=(own_half,))
    others = core_swap(others)
    second = [pull(first[k], z_source(k)) for k in range(4)]
    cut = cut_columns(info, tokens, [AWAY_AT + k for k in range(4)], ROWS, True, after=(first[0],))
    cut += cut_columns(info, tokens, [AWAY_AT + k for k in range(4, 8)], ROWS, True, after=(second[0],))
    arrived = [pull(cut[k], from_shard(-dy, dx)) if k else cut[k] for k, (dy, dx) in enumerate(AWAY)]

    mine, theirs = project(info, tokens, others, weight, first, second, arrived[1:8])
    key_grad = key_gradient(info, mine, core_swap(theirs), cotangent, gain[None], [])

    keys = {(0, 1): pull(key_grad, from_shard(0, 1))}
    for dy in (1, 3, 2):
        keys[dy, 0] = pull(key_grad, from_shard(dy, 0))
    keys[1, 1] = pull(keys[0, 1], from_shard(1, 0))
    keys[3, 1] = pull(keys[0, 1], from_shard(3, 0))
    keys[2, 1] = pull(keys[2, 0], from_shard(0, 1))

    mine, theirs = token_gradient(
        info, key_grad, core_swap(key_grad), weight, first, second,
        [keys[a] for a in ((0, 1), (1, 0), (3, 0), (2, 0))],
    )
    input_grad = place_columns(info, mine, core_swap(theirs))

    keys[0, 0] = key_grad
    blended, corner, quarter, *parts = blend(
        info, arrived, [keys[(-dy) % 4, dx] for dy, dx in AWAY], momentum, mask, tables, mine
    )
    residue = remove_corner(blended, corner, tables)

    def group_source(k):
        return lambda z, x, c, y: (z, x ^ (k // 2), c ^ (k % 2), y)

    def pull_z(value, flip):
        return pull(value, lambda z, x, c, y: (z ^ flip, x, c, y)).astype(f32)

    parts = {k: pull(parts[k - 1], group_source(k)) for k in (2, 3, 1)}
    summed = add_parts(quarter, [parts[k] for k in (1, 2, 3)], residue)
    summed = (summed.astype(f32) + pull_z(summed, 1)).astype(bf16)
    p4, p2, p6 = (pull_z(summed, flip) for flip in (4, 2, 6))
    summed = ((summed.astype(f32) + p2) + (p4 + p6)).astype(bf16)
    quarters = [summed] + [pull(summed, group_source(k)) for k in (1, 2, 3)]
    update = normalized_update(info, quarters, tables, ones, input_grad)
    return (input_grad[None], residue[None], update)


def solution(mesh):
    return jax.shard_map(
        per_device,
        mesh=mesh,
        in_specs=(
            P("rep", "shard", None),
            P("rep", "shard", None),
            P("shard", None),
            P("rep", "shard", None),
            P(),
            P(),
        ),
        out_specs=(P("rep", "shard", None), P("rep", "shard", None), P("shard", None)),
        check_vma=False,
    )
```
